32 devices in a mesh: parts: 2 (over x), seq: 16 (over z, y, core).
Axes of the slice: x: 2, y: 2, z: 4, core: 2. Of those that a mesh axis runs over, the one named last changes fastest.
Arguments:
- queries: bfloat16 [4096, 8192], P(('parts', 'seq')), parts along dimension 0, may hold values from -128 to 128
- keys: bfloat16 [4096, 1024], P(('parts', 'seq')), parts along dimension 0, may hold values from -6 to 6
- values: bfloat16 [4096, 1024], P(('parts', 'seq')), parts along dimension 0, may hold values from -6 to 6
- stream_block: int32 [256], P(('parts', 'seq')), parts along dimension 0, may hold values from 0 to 127, as said below
- segment_ids: int32 [4096], P('parts'), parts along dimension 0, may hold values from 0 to 3, never falling along the last dimension, each value on 1 to 1536 neighbouring positions
Outputs:
- attended: bfloat16 [4096, 8192], P(('parts', 'seq')), parts along dimension 0
The draws below stay inside these ranges and needn't reach their ends.
There are 2 independent parts, one for each index of `parts`. The reference program is written for one: setup_inputs(seed, part) draws one part's arguments, and reference() takes and returns one part's arrays. A program takes and returns all parts, laid end to end along the dimension named above; each array names one. Nothing has to cross between parts.
Inputs may be any that keep to these rules, and one draw needn't show every extreme that they name: `stream_block`: A permutation of the numbers of the 128 blocks. Block number b lies in the share of device floor(b / 8) of the joined sequences. The blocks loaded by one device land in the shares of 8 different devices, at most one block in each, and every device's share takes one block from each of 8 loading devices.
All inputs are finite; a program needn't handle non-finite values.
Results may differ from the reference program's by a relative error of at most 0.004.
Values may be sent and summed in bfloat16 or wider, within the bound.
A program may use at most 64 MiB of HBM per device.

```python
import math
import jax
import jax.numpy as jnp
import numpy as np
from jax import lax

H = 64
KVH = 8
HD = 128
TOK_DEV = 128
SEQS = 4
BLK = 16
TOKENS = 2048


def shared_keys(key):
    base = jnp.clip(jax.random.normal(key, (TOKENS, KVH * HD), jnp.float32), -6.0, 6.0)
    return base


def draw_keys(key, part):
    base = shared_keys(key)
    return base.astype(jnp.bfloat16)


def draw_queries(key, part):
    own_key = jax.random.fold_in(key, 5)
    result = jnp.clip(jax.random.normal(own_key, (TOKENS, H * HD), jnp.float32), -6.0, 6.0)
    return result.astype(jnp.bfloat16)


def slot_shuffle(subkey):
    return jax.random.permutation(subkey, TOK_DEV // BLK)


def draw_stream_block(key, part):
    own_key = jax.random.fold_in(key, 7)
    devices = TOKENS // TOK_DEV
    rounds = TOK_DEV // BLK
    key_offsets, key_source, key_target, key_slots = jax.random.split(own_key, 4)
    offsets = jax.random.permutation(key_offsets, devices)[:rounds]
    relabel_source = jax.random.permutation(key_source, devices)
    relabel_target = jax.random.permutation(key_target, devices)
    targets = relabel_target[(relabel_source[:, None] + offsets[None, :]) % devices]
    slot_table = jax.vmap(slot_shuffle)(jax.random.split(key_slots, devices))
    slots = slot_table[targets, jnp.arange(rounds, dtype=jnp.int32)[None, :]]
    return (targets * rounds + slots).reshape(-1).astype(jnp.int32)


def block_levels(key, dims, cuts, smallest, largest):
    level, own = 1.0, jax.random.fold_in(key, 6)
    for dim, blocks in cuts:
        heights = jnp.exp(jax.random.uniform(jax.random.fold_in(own, dim), (blocks,), jnp.float32, smallest / len(cuts), largest / len(cuts)))
        level = level * jnp.repeat(heights, dims[dim] // blocks).reshape([-1 if axis == dim else 1 for axis in range(len(dims))])
    return level


def split_up(number_of, total, most, lean):
    loads = [(1 << 20) // math.isqrt(grade ** lean) + 1 for grade in range(2, number_of + 1)]
    surplus, given = total - most - (number_of - 1), [1] * (number_of - 1)
    while surplus > 0:
        free = [i for i in range(number_of - 1) if given[i] < most]
        pool, remaining = sum([loads[i] for i in free]), surplus
        for i in free:
            more = min(most - given[i], max(1, remaining * loads[i] // pool), surplus)
            given[i] = given[i] + more
            surplus = surplus - more
    return np.array([most] + given)


def ragged(key, count, total, most, skew):
    if count == 2:
        one = jax.random.randint(key, (), max(1, total - most), min(most, total - 1) + 1)
        return jnp.stack([one, total - one])
    tallies = jnp.asarray(split_up(count, total, most, skew), jnp.int32)
    twos = (count - 1) // 2
    donor, taker = tallies[1:1 + 2 * twos:2], tallies[2:2 + 2 * twos:2]
    margin = jnp.minimum(donor - 1, most - taker)
    shifted = jax.random.randint(jax.random.fold_in(key, 1), (twos,), 0, 1 << 20) % (margin + 1)
    tallies = tallies.at[1:1 + 2 * twos:2].set(donor - shifted).at[2:2 + 2 * twos:2].set(taker + shifted)
    return tallies[jax.random.permutation(jax.random.fold_in(key, 2), count)]


def noise(key, extent, spread, limit, pieces=(), kind=jnp.bfloat16):
    loudness = block_levels(key, extent, pieces, -0.22, 0.18) if pieces else 1.0
    drawn = jax.random.normal(key, extent, jnp.float32) * spread * loudness
    return jnp.minimum(jnp.maximum(drawn, -limit), limit).astype(kind)


def setup_inputs(seed: int = 0, part: int = 0) -> dict:
    arg_keys = jax.random.split(jax.random.key(seed), 6)
    part_splits = jax.random.split(jax.random.fold_in(arg_keys[5], part), 6)
    queries = draw_queries(jax.random.fold_in(jax.random.fold_in(arg_keys[5], part), 71), part)
    keys = draw_keys(jax.random.fold_in(jax.random.fold_in(arg_keys[5], part), 71), part)
    values = noise(part_splits[2], (TOKENS, KVH * HD), 1.0, 6.0, ((0, 16),))
    stream_block = draw_stream_block(jax.random.fold_in(jax.random.fold_in(arg_keys[5], part), 71), part)
    segment_ids = jnp.searchsorted(jnp.cumsum(ragged(part_splits[4], SEQS, TOKENS, 3 * TOKENS // 4, 2)), jnp.arange(TOKENS), side="right").astype(jnp.int32)
    return {"queries": queries, "keys": keys, "values": values, "stream_block": stream_block, "segment_ids": segment_ids}


masked_floor = -1e30
query_block_rows = 512


def stream_order(stream_block):
    count = stream_block.shape[0]
    return jnp.zeros((count,), jnp.int32).at[stream_block].set(jnp.arange(count, dtype=jnp.int32))


def reorder(rows, indices):
    count = indices.shape[0]
    shaped = rows.reshape(count, rows.shape[0] // count, rows.shape[1])
    return shaped[indices].reshape(rows.shape)


def reference(queries, keys, values, stream_block, segment_ids):
    order = stream_order(stream_block)
    stream_queries = reorder(queries, order)
    stream_keys = reorder(keys, order)
    stream_values = reorder(values, order)
    total = queries.shape[0]
    group = H // KVH
    scale = HD ** -0.5
    places = jnp.arange(total, dtype=jnp.int32)
    tiles = total // query_block_rows

    def one_group(head_group):
        group_queries = lax.dynamic_slice_in_dim(stream_queries, head_group * (group * HD), group * HD, 1)
        group_keys = lax.dynamic_slice_in_dim(stream_keys, head_group * HD, HD, 1).astype(jnp.float32)
        group_values = lax.dynamic_slice_in_dim(stream_values, head_group * HD, HD, 1).astype(jnp.float32)

        def one_tile(tile_index):
            first = tile_index * query_block_rows
            block = lax.dynamic_slice_in_dim(group_queries, first, query_block_rows, 0)
            block = block.reshape(query_block_rows, group, HD).astype(jnp.float32)
            scores = jnp.einsum("qhd,kd->qhk", block, group_keys) * scale
            query_places = lax.dynamic_slice_in_dim(places, first, query_block_rows, 0)
            query_segments = lax.dynamic_slice_in_dim(segment_ids, first, query_block_rows, 0)
            allowed = (query_segments[:, None] == segment_ids[None, :]) & (places[None, :] <= query_places[:, None])
            masked = jnp.where(allowed[:, None, :], scores, masked_floor)
            highest = jnp.max(masked, axis=2, keepdims=True)
            rounded = jnp.where(allowed[:, None, :], jnp.exp(masked - highest), 0.0).astype(jnp.bfloat16)
            weights = lax.optimization_barrier(rounded).astype(jnp.float32)
            totals = jnp.sum(weights, axis=2)
            mixed = jnp.einsum("qhk,kd->qhd", weights, group_values)
            return (mixed / totals[:, :, None]).astype(jnp.bfloat16)

        return lax.map(one_tile, jnp.arange(tiles, dtype=jnp.int32))

    grouped = lax.map(one_group, jnp.arange(KVH, dtype=jnp.int32))
    attended_stream = jnp.transpose(grouped, (1, 2, 0, 3, 4)).reshape(total, H * HD)
    return reorder(attended_stream, stream_block)
```

```python
import functools

import jax
import jax.numpy as jnp
from jax import lax
from jax.experimental import pallas as pl
from jax.experimental.pallas import tpu as pltpu
from jax.sharding import PartitionSpec as P

KVH = 8
HD = 128
masked_floor = -1e30
log2_e = 1.4426950408889634


def attend_kernel(block_rows, q_ref, k_ref, v_ref, key_blocks_ref, own_places_ref, segments_ref, o_ref, bias_ref):
    rows = q_ref.shape[0]
    total = k_ref.shape[0]
    heads = q_ref.shape[1] // HD

    @pl.when(pl.program_id(0) == 0)
    def _():
        own = own_places_ref[...]
        segments = segments_ref[...]
        places = lax.broadcasted_iota(jnp.int32, (rows, total), 1)
        mine = jnp.sum(jnp.where(places == own, segments, 0), axis=1, keepdims=True)
        first = jnp.sum(jnp.where(segments < mine, 1, 0), axis=1, keepdims=True)
        key_places = key_blocks_ref[...]
        allowed = (key_places >= first) & (key_places <= own)
        bias_ref[...] = jnp.where(allowed, 0.0, masked_floor).astype(jnp.float32)

    keys = k_ref[...]
    values = jnp.concatenate([v_ref[...], jnp.ones_like(v_ref)], axis=1)
    factor = (HD ** -0.5) * log2_e
    for head in range(heads):
        columns = pl.ds(head * HD, HD)
        scores = lax.dot_general(
            q_ref[:, columns], keys, (((1,), (1,)), ((), ())), preferred_element_type=jnp.float32
        )
        scores = scores + bias_ref[...]
        highest = jnp.max(scores, axis=1, keepdims=True)
        weights = jnp.exp2((scores - highest) * factor).astype(jnp.bfloat16)
        mixed = jnp.dot(weights, values, preferred_element_type=jnp.float32)
        o_ref[:, columns] = (mixed[:, :HD] / mixed[:, HD:]).astype(o_ref.dtype)


def attend(queries, all_keys, all_values, key_places, own_places, segments, block_rows):
    rows, width = queries.shape
    total = all_keys.shape[0]
    group = width // KVH
    whole = lambda i: (0, 0)
    return pl.pallas_call(
        functools.partial(attend_kernel, block_rows),
        grid=(KVH,),
        out_shape=jax.ShapeDtypeStruct((rows, width), jnp.bfloat16),
        in_specs=[
            pl.BlockSpec((rows, group), lambda i: (0, i)),
            pl.BlockSpec((total, HD), lambda i: (0, i)),
            pl.BlockSpec((total, HD), lambda i: (0, i)),
            pl.BlockSpec((1, total), whole),
            pl.BlockSpec((rows, 1), whole),
            pl.BlockSpec((1, total), whole),
        ],
        out_specs=pl.BlockSpec((rows, group), lambda i: (0, i)),
        scratch_shapes=[pltpu.VMEM((rows, total), jnp.float32)],
        compiler_params=pltpu.CompilerParams(vmem_limit_bytes=56 * 1024 * 1024),
    )(queries, all_keys, all_values, key_places, own_places, segments)


def body(queries, keys, values, stream_block, segment_ids):
    rows = queries.shape[0]
    block_rows = rows // stream_block.shape[0]
    inside = jnp.arange(block_rows, dtype=jnp.int32)
    own = (stream_block[:, None] * block_rows + inside[None, :]).reshape(-1)
    key_places = lax.all_gather(own, "seq", axis=0, tiled=True)
    all_keys = lax.all_gather(keys, "seq", axis=0, tiled=True)
    all_values = lax.all_gather(values, "seq", axis=0, tiled=True)
    return attend(
        queries, all_keys, all_values, key_places[None, :], own[:, None], segment_ids[None, :], block_rows
    )


def solution(mesh):
    placed = (
        P(("parts", "seq"), None),
        P(("parts", "seq"), None),
        P(("parts", "seq"), None),
        P(("parts", "seq")),
        P("parts"),
    )
    return jax.shard_map(
        body, mesh=mesh, in_specs=placed, out_specs=P(("parts", "seq"), None), check_vma=False
    )
```

```python
import functools

import jax
import jax.numpy as jnp
from jax import lax
from jax.experimental import pallas as pl
from jax.experimental.pallas import tpu as pltpu
from jax.sharding import PartitionSpec as P

KVH = 8
HD = 128
masked_floor = -1e30
log2_e = 1.4426950408889634
factor = (HD ** -0.5) * log2_e

RK, RP, RV, LK, LP, LV, SK0, SP0, SV0, SK1, SP1, SV1 = range(12)


def ring_attend_kernel(
    chips, depth, q_ref, k_ref, v_ref, places_ref, own_ref, segments_ref, o_ref,
    k_buf, v_buf, p_buf, bias_ref, first_ref, acc_ref, sum_ref, top_ref, send_sem, recv_sem,
):
    rows = q_ref.shape[0]
    heads = q_ref.shape[1] // (KVH * HD)
    half = chips // 2

    me = lax.axis_index("seq")
    core = me % 2
    chip = me // 2
    columns = chips // depth
    z = chip // columns
    y = chip % columns
    place = z + y * (2 * depth - 1 - 2 * z)

    def device_at(ring_place):
        turn = ring_place // depth
        step = ring_place % depth
        return ((step + turn * (depth - 1 - 2 * step)) * columns + turn) * 2 + core

    right = device_at((place + 1) % chips)
    left = device_at((place + chips - 1) % chips)
    sibling = chip * 2 + 1 - core

    barrier = pltpu.get_barrier_semaphore()
    for peer in (right, left, sibling):
        pl.semaphore_signal(barrier, inc=1, device_id={"seq": peer}, device_id_type=pl.DeviceIdType.MESH)

    def part(buf, slot, quarter):
        if buf is p_buf:
            return p_buf.at[slot, quarter]
        return buf.at[slot, pl.ds(quarter * rows, rows)]

    def copy(kind, buf, source, target, peer):
        return pltpu.make_async_remote_copy(
            src_ref=part(buf, *source),
            dst_ref=part(buf, *target),
            send_sem=send_sem.at[kind, target[0]],
            recv_sem=recv_sem.at[kind, target[0]],
            device_id={"seq": peer},
            device_id_type=pl.DeviceIdType.MESH,
        )

    def follow(slot, quarter, last, buf):
        which = 0 if buf is k_buf else 1 if buf is p_buf else 2
        origin = isinstance(slot, int) and slot == 0
        final = isinstance(slot, int) and slot == half
        out = []
        if not final:
            if quarter == 0 and (buf is not v_buf or not last):
                out.append(((RK, RP, RV)[which], buf, (slot, 0), (slot + 1, 0), right))
            if (quarter == 1 or origin) and (buf is v_buf or not last):
                out.append(((LK, LP, LV)[which], buf, (slot, quarter), (slot + 1, 0 if last else 1), left))
        if origin or final:
            out.append(((SK0, SP0, SV0)[which], buf, (slot, 0), (slot, 1), sibling))
        else:
            kinds = (SK0, SP0, SV0) if quarter == 0 else (SK1, SP1, SV1)
            out.append((kinds[which], buf, (slot, quarter), (slot, quarter + 2), sibling))
        return out

    def wait_for(kind, buf, slot, quarter):
        copy(kind, buf, (slot, quarter), (slot, quarter), sibling).wait_recv()

    def arrive(slot, last):
        for buf, right_kind, left_kind in ((k_buf, RK, LK), (p_buf, RP, LP), (v_buf, RV, LV)):
            for kind, quarter in ((right_kind, 0), (left_kind, 1)):
                wait_for(kind, buf, slot, quarter)
                for item in follow(slot, quarter, last, buf):
                    copy(*item).start()
        for buf, kinds in ((k_buf, (SK0, SK1)), (p_buf, (SP0, SP1)), (v_buf, (SV0, SV1))):
            wait_for(kinds[0], buf, slot, 2)
            wait_for(kinds[1], buf, slot, 3)

    def sent(slot, quarters, last):
        for buf in (k_buf, p_buf, v_buf):
            for quarter in quarters:
                for item in follow(slot, quarter, last, buf):
                    copy(*item).wait_send()

    def compute(slot, parts, opening, closing):
        width = parts * rows
        key_places = jnp.concatenate([p_buf[slot, n][0:1, :] for n in range(parts)], axis=1)
        allowed = (key_places >= first_ref[...]) & (key_places <= own_ref[...])
        bias_ref[:, 0:width] = jnp.where(allowed, 0.0, masked_floor).astype(jnp.float32)

        def key_head(index, carry):
            columns = pl.ds(pl.multiple_of(index * HD, HD), HD)
            keys = k_buf[slot, 0:width, columns]
            values = v_buf[slot, 0:width, columns]
            values = jnp.concatenate([values, jnp.ones_like(values)], axis=1)
            for head in range(heads):
                here = pl.ds(pl.multiple_of((index * heads + head) * HD, HD), HD)
                scores = lax.dot_general(
                    q_ref[:, here], keys, (((1,), (1,)), ((), ())), preferred_element_type=jnp.float32
                )
                scores = scores + bias_ref[:, 0:width]
                highest = jnp.max(scores, axis=1, keepdims=True)
                if opening:
                    top = jnp.broadcast_to(highest, (rows, HD))
                else:
                    before = top_ref[:, here]
                    top = jnp.maximum(before, highest)
                wide = jnp.concatenate([top] * (width // HD), axis=1)
                weights = jnp.exp2((scores - wide) * factor).astype(jnp.bfloat16)
                mixed = jnp.dot(weights, values, preferred_element_type=jnp.float32)
                acc, total = mixed[:, :HD], mixed[:, HD:]
                if not opening:
                    shrink = jnp.exp2((before - top) * factor)
                    acc = acc_ref[:, here] * shrink + acc
                    total = sum_ref[:, here] * shrink + total
                if closing:
                    o_ref[:, here] = (acc / total).astype(o_ref.dtype)
                else:
                    acc_ref[:, here] = acc
                    sum_ref[:, here] = total
                    top_ref[:, here] = top
            return carry

        lax.fori_loop(0, KVH, key_head, 0)

    k_buf[0, 0:rows, :] = k_ref[...]
    v_buf[0, 0:rows, :] = v_ref[...]
    p_buf[0, 0] = places_ref[...]
    pl.semaphore_wait(barrier, 3)
    for buf in (k_buf, p_buf, v_buf):
        for item in follow(0, 0, False, buf):
            copy(*item).start()

    own = own_ref[...]
    segments = segments_ref[...]
    spots = lax.broadcasted_iota(jnp.int32, (rows, segments.shape[1]), 1)
    mine = jnp.sum(jnp.where(spots == own, segments, 0), axis=1, keepdims=True)
    first_ref[...] = jnp.sum(jnp.where(segments < mine, 1, 0), axis=1, keepdims=True)

    wait_for(SK0, k_buf, 0, 1)
    wait_for(SP0, p_buf, 0, 1)
    wait_for(SV0, v_buf, 0, 1)
    compute(0, 2, True, False)

    def middle(slot, carry):
        arrive(slot, False)
        compute(slot, 4, False, False)
        return carry

    lax.fori_loop(1, half - 1, middle, 0)
    arrive(half - 1, True)
    compute(half - 1, 4, False, False)

    for buf, kind in ((k_buf, RK), (p_buf, RP), (v_buf, LV)):
        wait_for(kind, buf, half, 0)
        for item in follow(half, 0, False, buf):
            copy(*item).start()
    wait_for(SK0, k_buf, half, 1)
    wait_for(SP0, p_buf, half, 1)
    wait_for(SV0, v_buf, half, 1)
    compute(half, 2, False, True)

    sent(0, (0,), False)

    def settle(slot, carry):
        sent(slot, (0, 1), False)
        return carry

    lax.fori_loop(1, half - 1, settle, 0)
    sent(half - 1, (0, 1), True)
    sent(half, (0,), False)


def ring_attend(queries, keys, values, places, own_places, segments, chips, depth):
    rows, width = queries.shape
    slots = chips // 2 + 1
    vmem = pl.BlockSpec(memory_space=pltpu.VMEM)
    return pl.pallas_call(
        functools.partial(ring_attend_kernel, chips, depth),
        out_shape=jax.ShapeDtypeStruct((rows, width), jnp.bfloat16),
        in_specs=[vmem] * 6,
        out_specs=vmem,
        scratch_shapes=[
            pltpu.VMEM((slots, 4 * rows, keys.shape[1]), jnp.bfloat16),
            pltpu.VMEM((slots, 4 * rows, keys.shape[1]), jnp.bfloat16),
            pltpu.VMEM((slots, 4, 8, rows), jnp.int32),
            pltpu.VMEM((rows, 4 * rows), jnp.float32),
            pltpu.VMEM((rows, 1), jnp.int32),
            pltpu.VMEM((rows, width), jnp.float32),
            pltpu.VMEM((rows, width), jnp.float32),
            pltpu.VMEM((rows, width), jnp.float32),
            pltpu.SemaphoreType.DMA((12, slots)),
            pltpu.SemaphoreType.DMA((12, slots)),
        ],
        compiler_params=pltpu.CompilerParams(
            collective_id=0, has_side_effects=True, vmem_limit_bytes=60 * 1024 * 1024
        ),
    )(queries, keys, values, places, own_places, segments)


def body(queries, keys, values, stream_block, segment_ids):
    rows = queries.shape[0]
    block_rows = rows // stream_block.shape[0]
    inside = jnp.arange(block_rows, dtype=jnp.int32)
    own = (stream_block[:, None] * block_rows + inside[None, :]).reshape(-1)
    chips = lax.axis_size("seq") // 2
    depth = chips // 2 if lax.axis_size("parts") == 2 else chips
    places = jnp.broadcast_to(own[None, :], (8, rows))
    return ring_attend(
        queries, keys, values, places, own[:, None], segment_ids[None, :], chips, depth
    )


def solution(mesh):
    placed = (
        P(("parts", "seq"), None),
        P(("parts", "seq"), None),
        P(("parts", "seq"), None),
        P(("parts", "seq")),
        P("parts"),
    )
    return jax.shard_map(
        body, mesh=mesh, in_specs=placed, out_specs=P(("parts", "seq"), None), check_vma=False
    )
```

```python
import functools

import jax
import jax.numpy as jnp
from jax import lax
from jax.experimental import pallas as pl
from jax.experimental.pallas import tpu as pltpu
from jax.sharding import PartitionSpec as P

KVH = 8
HD = 128
masked_floor = -1e30
log2_e = 1.4426950408889634
factor = (HD ** -0.5) * log2_e

RK, RP, RV, LK, LP, LV, SK0, SP0, SV0, SK1, SP1, SV1 = range(12)


def ring_attend_kernel(
    chips, depth, q_ref, k_ref, v_ref, blocks_ref, segments_ref, o_ref,
    k_buf, v_buf, p_buf, bias_ref, first_ref, acc_ref, sum_ref, top_ref, send_sem, recv_sem,
):
    rows = q_ref.shape[0]
    heads = q_ref.shape[1] // (KVH * HD)
    half = chips // 2

    me = lax.axis_index("seq")
    core = me % 2
    chip = me // 2
    columns = chips // depth
    z = chip // columns
    y = chip % columns
    place = z + y * (2 * depth - 1 - 2 * z)

    def device_at(ring_place):
        turn = ring_place // depth
        step = ring_place % depth
        return ((step + turn * (depth - 1 - 2 * step)) * columns + turn) * 2 + core

    right = device_at((place + 1) % chips)
    left = device_at((place + chips - 1) % chips)
    sibling = chip * 2 + 1 - core

    barrier = pltpu.get_barrier_semaphore()
    for peer in (right, left, sibling):
        pl.semaphore_signal(barrier, inc=1, device_id={"seq": peer}, device_id_type=pl.DeviceIdType.MESH)

    def part(buf, slot, quarter):
        if buf is p_buf:
            return p_buf.at[slot, quarter]
        return buf.at[slot, pl.ds(quarter * rows, rows)]

    def copy(kind, buf, source, target, peer):
        return pltpu.make_async_remote_copy(
            src_ref=part(buf, *source),
            dst_ref=part(buf, *target),
            send_sem=send_sem.at[kind, target[0]],
            recv_sem=recv_sem.at[kind, target[0]],
            device_id={"seq": peer},
            device_id_type=pl.DeviceIdType.MESH,
        )

    def follow(slot, quarter, last, buf):
        which = 0 if buf is k_buf else 1 if buf is p_buf else 2
        origin = isinstance(slot, int) and slot == 0
        final = isinstance(slot, int) and slot == half
        out = []
        if not final:
            if quarter == 0 and (buf is not v_buf or not last):
                out.append(((RK, RP, RV)[which], buf, (slot, 0), (slot + 1, 0), right))
            if (quarter == 1 or origin) and (buf is v_buf or not last):
                out.append(((LK, LP, LV)[which], buf, (slot, quarter), (slot + 1, 0 if last else 1), left))
        if origin or final:
            out.append(((SK0, SP0, SV0)[which], buf, (slot, 0), (slot, 1), sibling))
        else:
            kinds = (SK0, SP0, SV0) if quarter == 0 else (SK1, SP1, SV1)
            out.append((kinds[which], buf, (slot, quarter), (slot, quarter + 2), sibling))
        return out

    def wait_for(kind, buf, slot, quarter):
        copy(kind, buf, (slot, quarter), (slot, quarter), sibling).wait_recv()

    def arrive(slot, last):
        for buf, right_kind, left_kind in ((k_buf, RK, LK), (p_buf, RP, LP), (v_buf, RV, LV)):
            for kind, quarter in ((right_kind, 0), (left_kind, 1)):
                wait_for(kind, buf, slot, quarter)
                for item in follow(slot, quarter, last, buf):
                    copy(*item).start()
        for buf, kinds in ((k_buf, (SK0, SK1)), (p_buf, (SP0, SP1)), (v_buf, (SV0, SV1))):
            wait_for(kinds[0], buf, slot, 2)
            wait_for(kinds[1], buf, slot, 3)

    def sent(slot, quarters, last):
        for buf in (k_buf, p_buf, v_buf):
            for quarter in quarters:
                for item in follow(slot, quarter, last, buf):
                    copy(*item).wait_send()

    def compute(slot, parts, opening, closing):
        width = parts * rows
        for n in range(parts):
            key_places = jnp.transpose(jnp.broadcast_to(p_buf[slot, n][0:1, :], (rows, rows)))
            allowed = (key_places >= first_ref[0:1, :]) & (key_places <= p_buf[0, 0][0:1, :])
            bias_ref[n * rows : (n + 1) * rows, :] = jnp.where(allowed, 0.0, masked_floor).astype(jnp.float32)

        def key_head(index, carry):
            columns = pl.ds(pl.multiple_of(index * HD, HD), HD)
            keys = k_buf[slot, 0:width, columns]
            values = jnp.transpose(v_buf[slot, 0:width, columns])
            values = jnp.concatenate([values, jnp.ones((16, width), jnp.bfloat16)], axis=0)
            for n in range(heads // 2):
                pair = index * (heads // 2) + n
                one = pl.ds(pl.multiple_of(pair * 2 * HD, HD), HD)
                two = pl.ds(pl.multiple_of(pair * 2 * HD + HD, HD), HD)
                asked = jnp.concatenate([q_ref[:, one], q_ref[:, two]], axis=0)
                scores = lax.dot_general(
                    keys, asked, (((1,), (1,)), ((), ())), preferred_element_type=jnp.float32
                )
                bias = bias_ref[0:width, :]
                scores = scores + jnp.concatenate([bias, bias], axis=1)
                top = jnp.max(scores, axis=0, keepdims=True)
                if not opening:
                    before = top_ref[pair]
                    top = jnp.maximum(before, top)
                weights = jnp.exp2((scores - top) * factor).astype(jnp.bfloat16)
                mixed = jnp.dot(values, weights, preferred_element_type=jnp.float32)
                acc, total = mixed[:HD, :], mixed[HD : HD + 1, :]
                if not opening:
                    shrink = jnp.exp2((before - top) * factor)
                    acc = acc_ref[pair] * shrink + acc
                    total = sum_ref[pair] * shrink + total
                if closing:
                    done = (acc / total).astype(o_ref.dtype)
                    o_ref[:, one] = jnp.transpose(done[:, :rows])
                    o_ref[:, two] = jnp.transpose(done[:, rows:])
                else:
                    acc_ref[pair] = acc
                    sum_ref[pair] = total
                    top_ref[pair] = top
            return carry

        lax.fori_loop(0, KVH, key_head, 0)

    k_buf[0, 0:rows, :] = k_ref[...]
    v_buf[0, 0:rows, :] = v_ref[...]
    blocks = blocks_ref.shape[0]
    block_rows = rows // blocks
    lane = lax.broadcasted_iota(jnp.int32, (8, rows), 1)
    where_from = lane * 0
    for n in range(blocks):
        where_from = jnp.where(
            (lane >= n * block_rows) & (lane < (n + 1) * block_rows),
            lane + (blocks_ref[n] - n) * block_rows,
            where_from,
        )
    p_buf[0, 0] = where_from
    pl.semaphore_wait(barrier, 3)
    for buf in (k_buf, p_buf, v_buf):
        for item in follow(0, 0, False, buf):
            copy(*item).start()

    own = jnp.transpose(jnp.broadcast_to(where_from[0:1, :], (rows, rows)))[:, 0:1]
    segments = segments_ref[...]
    spots = lax.broadcasted_iota(jnp.int32, (rows, segments.shape[1]), 1)
    mine = jnp.sum(jnp.where(spots == own, segments, 0), axis=1, keepdims=True)
    first = jnp.sum(jnp.where(segments < mine, 1, 0), axis=1, keepdims=True)
    first_ref[...] = jnp.transpose(jnp.broadcast_to(first, (rows, rows)))[0:8, :]

    wait_for(SK0, k_buf, 0, 1)
    wait_for(SP0, p_buf, 0, 1)
    wait_for(SV0, v_buf, 0, 1)
    compute(0, 2, True, False)

    def middle(slot, carry):
        arrive(slot, False)
        compute(slot, 4, False, False)
        return carry

    lax.fori_loop(1, half - 1, middle, 0)
    arrive(half - 1, True)
    compute(half - 1, 4, False, False)

    for buf, kind in ((k_buf, RK), (p_buf, RP), (v_buf, LV)):
        wait_for(kind, buf, half, 0)
        for item in follow(half, 0, False, buf):
            copy(*item).start()
    wait_for(SK0, k_buf, half, 1)
    wait_for(SP0, p_buf, half, 1)
    wait_for(SV0, v_buf, half, 1)
    compute(half, 2, False, True)

    sent(0, (0,), False)

    def settle(slot, carry):
        sent(slot, (0, 1), False)
        return carry

    lax.fori_loop(1, half - 1, settle, 0)
    sent(half - 1, (0, 1), True)
    sent(half, (0,), False)


def ring_attend(queries, keys, values, blocks, segments, chips, depth):
    rows, width = queries.shape
    slots = chips // 2 + 1
    vmem = pl.BlockSpec(memory_space=pltpu.VMEM)
    return pl.pallas_call(
        functools.partial(ring_attend_kernel, chips, depth),
        out_shape=jax.ShapeDtypeStruct((rows, width), jnp.bfloat16),
        in_specs=[vmem] * 3 + [pl.BlockSpec(memory_space=pltpu.SMEM), vmem],
        out_specs=vmem,
        scratch_shapes=[
            pltpu.VMEM((slots, 4 * rows, keys.shape[1]), jnp.bfloat16),
            pltpu.VMEM((slots, 4 * rows, keys.shape[1]), jnp.bfloat16),
            pltpu.VMEM((slots, 4, 8, rows), jnp.int32),
            pltpu.VMEM((4 * rows, rows), jnp.float32),
            pltpu.VMEM((8, rows), jnp.int32),
            pltpu.VMEM((width // (2 * HD), HD, 2 * rows), jnp.float32),
            pltpu.VMEM((width // (2 * HD), 1, 2 * rows), jnp.float32),
            pltpu.VMEM((width // (2 * HD), 1, 2 * rows), jnp.float32),
            pltpu.SemaphoreType.DMA((12, slots)),
            pltpu.SemaphoreType.DMA((12, slots)),
        ],
        compiler_params=pltpu.CompilerParams(
            collective_id=0, has_side_effects=True, vmem_limit_bytes=60 * 1024 * 1024
        ),
    )(queries, keys, values, blocks, segments)


def body(queries, keys, values, stream_block, segment_ids):
    chips = lax.axis_size("seq") // 2
    depth = chips // 2 if lax.axis_size("parts") == 2 else chips
    return ring_attend(
        queries, keys, values, stream_block, segment_ids[None, :], chips, depth
    )


def solution(mesh):
    placed = (
        P(("parts", "seq"), None),
        P(("parts", "seq"), None),
        P(("parts", "seq"), None),
        P(("parts", "seq")),
        P("parts"),
    )
    return jax.shard_map(
        body, mesh=mesh, in_specs=placed, out_specs=P(("parts", "seq"), None), check_vma=False
    )
```

```python
import functools

import jax
import jax.numpy as jnp
from jax import lax
from jax.experimental import pallas as pl
from jax.experimental.pallas import tpu as pltpu
from jax.sharding import PartitionSpec as P

KVH = 8
HD = 128
masked_floor = -1e30
log2_e = 1.4426950408889634
factor = (HD ** -0.5) * log2_e
together = 2

RK, RP, RV, LK, LP, LV, SK0, SP0, SV0, SK1, SP1, SV1 = range(12)


def ring_attend_kernel(
    chips, depth, q_ref, k_ref, v_ref, blocks_ref, segments_ref, o_ref,
    k_buf, v_buf, p_buf, bias_ref, first_ref, own_ref, acc_ref, sum_ref, top_ref, send_sem, recv_sem,
):
    rows = q_ref.shape[0]
    heads = q_ref.shape[1] // (KVH * HD)
    half = chips // 2

    me = lax.axis_index("seq")
    core = me % 2
    chip = me // 2
    columns = chips // depth
    z = chip // columns
    y = chip % columns
    place = z + y * (2 * depth - 1 - 2 * z)

    def device_at(ring_place):
        turn = ring_place // depth
        step = ring_place % depth
        return ((step + turn * (depth - 1 - 2 * step)) * columns + turn) * 2 + core

    right = device_at((place + 1) % chips)
    left = device_at((place + chips - 1) % chips)
    sibling = chip * 2 + 1 - core

    barrier = pltpu.get_barrier_semaphore()
    for peer in (right, left, sibling):
        pl.semaphore_signal(barrier, inc=1, device_id={"seq": peer}, device_id_type=pl.DeviceIdType.MESH)

    def part(buf, slot, quarter):
        if buf is p_buf:
            return p_buf.at[slot, quarter]
        return buf.at[slot, pl.ds(quarter * rows, rows)]

    def copy(kind, buf, source, target, peer):
        return pltpu.make_async_remote_copy(
            src_ref=part(buf, *source),
            dst_ref=part(buf, *target),
            send_sem=send_sem.at[kind, target[0]],
            recv_sem=recv_sem.at[kind, target[0]],
            device_id={"seq": peer},
            device_id_type=pl.DeviceIdType.MESH,
        )

    def follow(slot, quarter, last, buf):
        which = 0 if buf is k_buf else 1 if buf is p_buf else 2
        origin = isinstance(slot, int) and slot == 0
        final = isinstance(slot, int) and slot == half
        out = []
        if not final:
            if quarter == 0 and (buf is not v_buf or not last):
                out.append(((RK, RP, RV)[which], buf, (slot, 0), (slot + 1, 0), right))
            if (quarter == 1 or origin) and (buf is v_buf or not last):
                out.append(((LK, LP, LV)[which], buf, (slot, quarter), (slot + 1, 0 if last else 1), left))
        if origin or final:
            out.append(((SK0, SP0, SV0)[which], buf, (slot, 0), (slot, 1), sibling))
        else:
            kinds = (SK0, SP0, SV0) if quarter == 0 else (SK1, SP1, SV1)
            out.append((kinds[which], buf, (slot, quarter), (slot, quarter + 2), sibling))
        return out

    def wait_for(kind, buf, slot, quarter):
        copy(kind, buf, (slot, quarter), (slot, quarter), sibling).wait_recv()

    def take(slot, last, entries):
        for buf, right_kind, left_kind in entries:
            for kind, quarter in ((right_kind, 0), (left_kind, 1)):
                wait_for(kind, buf, slot, quarter)
                for item in follow(slot, quarter, last, buf):
                    copy(*item).start()

    def arrive_keys(slot, last):
        take(slot, last, ((k_buf, RK, LK), (p_buf, RP, LP)))

    def arrive_values(slot, last):
        take(slot, last, ((v_buf, RV, LV),))
        for buf, kinds in ((k_buf, (SK0, SK1)), (p_buf, (SP0, SP1)), (v_buf, (SV0, SV1))):
            wait_for(kinds[0], buf, slot, 2)
            wait_for(kinds[1], buf, slot, 3)

    def arrive_last(buf, kind):
        wait_for(kind, buf, half, 0)
        for item in follow(half, 0, False, buf):
            copy(*item).start()

    def sent(slot, quarters, last):
        for buf in (k_buf, p_buf, v_buf):
            for quarter in quarters:
                for item in follow(slot, quarter, last, buf):
                    copy(*item).wait_send()

    def compute(slot, parts, opening, closing, begin=0, end=KVH):
        width = parts * rows
        if begin == 0:
            key_places = jnp.concatenate([p_buf[slot, n][0:1, :] for n in range(parts)], axis=1)
            allowed = (key_places >= first_ref[...]) & (key_places <= own_ref[...])
            bias_ref[:, 0:width] = jnp.where(allowed, 0.0, masked_floor).astype(jnp.float32)

        def key_head(index, carry):
            columns = pl.ds(pl.multiple_of(index * HD, HD), HD)
            keys = k_buf[slot, 0:width, columns]
            values = v_buf[slot, 0:width, columns]
            values = jnp.concatenate([values, jnp.ones_like(values)], axis=1)
            for start in range(0, heads, together):
                spots = [
                    pl.ds(pl.multiple_of((index * heads + start + n) * HD, HD), HD) for n in range(together)
                ]
                asked = jnp.concatenate([q_ref[:, spot] for spot in spots], axis=0)
                scores = lax.dot_general(
                    asked, keys, (((1,), (1,)), ((), ())), preferred_element_type=jnp.float32
                )
                weights, olds, tops = [], [], []
                for n, spot in enumerate(spots):
                    mine = scores[n * rows : (n + 1) * rows] + bias_ref[:, 0:width]
                    highest = jnp.max(mine, axis=1, keepdims=True)
                    if opening:
                        top = jnp.broadcast_to(highest, (rows, HD))
                    else:
                        olds.append(top_ref[:, spot])
                        top = jnp.maximum(olds[n], highest)
                    tops.append(top)
                    wide = jnp.concatenate([top] * (width // HD), axis=1)
                    weights.append(jnp.exp2((mine - wide) * factor).astype(jnp.bfloat16))
                mixed = jnp.dot(
                    jnp.concatenate(weights, axis=0), values, preferred_element_type=jnp.float32
                )
                for n, spot in enumerate(spots):
                    acc = mixed[n * rows : (n + 1) * rows, :HD]
                    total = mixed[n * rows : (n + 1) * rows, HD:]
                    if not opening:
                        shrink = jnp.exp2((olds[n] - tops[n]) * factor)
                        acc = acc_ref[:, spot] * shrink + acc
                        total = sum_ref[:, spot] * shrink + total
                    if closing:
                        o_ref[:, spot] = (acc / total).astype(o_ref.dtype)
                    else:
                        acc_ref[:, spot] = acc
                        sum_ref[:, spot] = total
                        top_ref[:, spot] = tops[n]
            return carry

        lax.fori_loop(begin, end, key_head, 0)

    k_buf[0, 0:rows, :] = k_ref[...]
    v_buf[0, 0:rows, :] = v_ref[...]
    blocks = blocks_ref.shape[0]
    block_rows = rows // blocks
    lane = lax.broadcasted_iota(jnp.int32, (8, rows), 1)
    where_from = lane * 0
    for n in range(blocks):
        where_from = jnp.where(
            (lane >= n * block_rows) & (lane < (n + 1) * block_rows),
            lane + (blocks_ref[n] - n) * block_rows,
            where_from,
        )
    p_buf[0, 0] = where_from
    pl.semaphore_wait(barrier, 3)
    for buf in (k_buf, p_buf, v_buf):
        for item in follow(0, 0, False, buf):
            copy(*item).start()

    own = jnp.transpose(jnp.broadcast_to(where_from[0:1, :], (rows, rows)))[:, 0:1]
    segments = segments_ref[...]
    spots = lax.broadcasted_iota(jnp.int32, (rows, segments.shape[1]), 1)
    mine = jnp.sum(jnp.where(spots == own, segments, 0), axis=1, keepdims=True)
    first_ref[...] = jnp.sum(jnp.where(segments < mine, 1, 0), axis=1, keepdims=True)
    own_ref[...] = own

    wait_for(SK0, k_buf, 0, 1)
    wait_for(SP0, p_buf, 0, 1)
    wait_for(SV0, v_buf, 0, 1)
    compute(0, 2, True, False)
    arrive_keys(1, False)
    arrive_values(1, False)

    def advance(slot, last):
        compute(slot, 4, False, False, 0, KVH // 2)
        arrive_keys(slot + 1, last)
        compute(slot, 4, False, False, KVH // 2, KVH)
        arrive_values(slot + 1, last)

    def middle(slot, carry):
        advance(slot, False)
        return carry

    lax.fori_loop(1, half - 2, middle, 0)
    advance(half - 2, True)

    compute(half - 1, 4, False, False, 0, KVH // 2)
    arrive_last(k_buf, RK)
    arrive_last(p_buf, RP)
    compute(half - 1, 4, False, False, KVH // 2, KVH)
    arrive_last(v_buf, LV)
    wait_for(SK0, k_buf, half, 1)
    wait_for(SP0, p_buf, half, 1)
    wait_for(SV0, v_buf, half, 1)
    compute(half, 2, False, True)

    sent(0, (0,), False)

    def settle(slot, carry):
        sent(slot, (0, 1), False)
        return carry

    lax.fori_loop(1, half - 1, settle, 0)
    sent(half - 1, (0, 1), True)
    sent(half, (0,), False)


def ring_attend(queries, keys, values, blocks, segments, chips, depth):
    rows, width = queries.shape
    slots = chips // 2 + 1
    vmem = pl.BlockSpec(memory_space=pltpu.VMEM)
    return pl.pallas_call(
        functools.partial(ring_attend_kernel, chips, depth),
        out_shape=jax.ShapeDtypeStruct((rows, width), jnp.bfloat16),
        in_specs=[vmem] * 3 + [pl.BlockSpec(memory_space=pltpu.SMEM), vmem],
        out_specs=vmem,
        scratch_shapes=[
            pltpu.VMEM((slots, 4 * rows, keys.shape[1]), jnp.bfloat16),
            pltpu.VMEM((slots, 4 * rows, keys.shape[1]), jnp.bfloat16),
            pltpu.VMEM((slots, 4, 8, rows), jnp.int32),
            pltpu.VMEM((rows, 4 * rows), jnp.float32),
            pltpu.VMEM((rows, 1), jnp.int32),
            pltpu.VMEM((rows, 1), jnp.int32),
            pltpu.VMEM((rows, width), jnp.float32),
            pltpu.VMEM((rows, width), jnp.float32),
            pltpu.VMEM((rows, width), jnp.float32),
            pltpu.SemaphoreType.DMA((12, slots)),
            pltpu.SemaphoreType.DMA((12, slots)),
        ],
        compiler_params=pltpu.CompilerParams(
            collective_id=0, has_side_effects=True, vmem_limit_bytes=60 * 1024 * 1024
        ),
    )(queries, keys, values, blocks, segments)


def body(queries, keys, values, stream_block, segment_ids):
    chips = lax.axis_size("seq") // 2
    depth = chips // 2 if lax.axis_size("parts") == 2 else chips
    return ring_attend(
        queries, keys, values, stream_block, segment_ids[None, :], chips, depth
    )


def solution(mesh):
    placed = (
        P(("parts", "seq"), None),
        P(("parts", "seq"), None),
        P(("parts", "seq"), None),
        P(("parts", "seq")),
        P("parts"),
    )
    return jax.shard_map(
        body, mesh=mesh, in_specs=placed, out_specs=P(("parts", "seq"), None), check_vma=False
    )
```
